32 devices in a mesh: rep: 2 (over y), row: 8 (over z, core), col: 2 (over x).
Axes of the slice: x: 2, y: 2, z: 4, core: 2. Of those that a mesh axis runs over, the one named last changes fastest.
Arguments:
- pair: bfloat16 [448, 224, 128], P(('rep', 'row'), 'col'), parts along dimension 0, may hold values from -6 to 6
- tri_gains: float32 [2, 2, 128], replicated, may hold values from 0.25 to 1.75
- tri_proj: bfloat16 [2, 5, 128, 128], replicated, may hold values from -0.5 to 0.5
- tri_out: bfloat16 [2, 128, 128], replicated, may hold values from -0.5 to 0.5
- trans_gain: float32 [128], replicated, may hold values from 0.25 to 1.75
- trans_up: bfloat16 [2, 128, 512], replicated, may hold values from -0.5 to 0.5
- trans_down: bfloat16 [512, 128], replicated, may hold values from -0.25 to 0.25
Outputs:
- pair_out: bfloat16 [448, 224, 128], P(('rep', 'row'), 'col'), parts along dimension 0
The draws below stay inside these ranges and needn't reach their ends.
There are 2 independent parts, one for each index of `rep`. The reference program is written for one: setup_inputs(seed, part) draws one part's arguments, and reference() takes and returns one part's arrays. A program takes and returns all parts, laid end to end along the dimension named above; an argument that names none is the same for every part. Nothing has to cross between parts.
All inputs are finite; a program needn't handle non-finite values.
Results may differ from the reference program's by a relative error of at most 0.018.
Values may be sent and summed in bfloat16 or wider, within the bound.
A program may use at most 128 MiB of HBM per device.

```python
import jax
import jax.numpy as jnp
from jax import lax

C = 128
TRANS = 512
TOKENS = 224


def levels(rng, extent, shards, least, high):
    factor_of = 1.0
    for axis_at, parts in shards:
        heights = jax.random.uniform(jax.random.fold_in(jax.random.fold_in(rng, 6), axis_at), (parts,), jnp.float32, least / len(shards), high / len(shards))
        factor_of = factor_of * jnp.repeat(jnp.exp(heights), extent[axis_at] // parts).reshape((-1,) + (1,) * (len(extent) - 1 - axis_at))
    return factor_of


def scatter_about(own_key, extent, scale, most, split=(), kind=jnp.bfloat16):
    drawn = scale * jax.random.normal(own_key, extent, jnp.float32)
    if split:
        drawn = drawn * levels(own_key, extent, split, -0.22, 0.18)
    return jnp.clip(drawn, -most, most).astype(kind)


def setup_inputs(seed: int = 0, part: int = 0) -> dict:
    splits = jax.random.split(jax.random.key(seed), 8)
    own_keys = jax.random.split(jax.random.fold_in(splits[7], part), 8)
    return {
        "pair": scatter_about(own_keys[0], (TOKENS, TOKENS, C), 1.0, 6.0, ((0, 8), (1, 2))),
        "tri_gains": jnp.clip(1.0 + 0.15 * jax.random.normal(splits[1], (2, 2, C), jnp.float32), 0.25, 1.75),
        "tri_proj": scatter_about(splits[2], (2, 5, C, C), C ** -0.5, 0.5),
        "tri_out": scatter_about(splits[3], (2, C, C), C ** -0.5, 0.5),
        "trans_gain": jnp.clip(1.0 + 0.15 * jax.random.normal(splits[4], (C,), jnp.float32), 0.25, 1.75),
        "trans_up": scatter_about(splits[5], (2, C, TRANS), C ** -0.5, 0.5),
        "trans_down": scatter_about(splits[6], (TRANS, C), TRANS ** -0.5, 0.25),
    }


def normalize(values, gain):
    mean = lax.optimization_barrier(jnp.mean(values, axis=-1, keepdims=True))
    centered = values - mean
    variance = lax.optimization_barrier(jnp.mean(centered * centered, axis=-1, keepdims=True))
    return centered * lax.rsqrt(variance + 1e-05) * gain

def project(flat, weight):
    return jnp.dot(flat, weight, preferred_element_type=jnp.float32)

def prepare(pair, gains, weights):
    tokens, width = (pair.shape[0], pair.shape[2])
    flat = normalize(pair.reshape(-1, width).astype(jnp.float32), gains[0]).astype(jnp.bfloat16)
    left = (jax.nn.sigmoid(project(flat, weights[1])) * project(flat, weights[0])).astype(jnp.bfloat16)
    right = (jax.nn.sigmoid(project(flat, weights[3])) * project(flat, weights[2])).astype(jnp.bfloat16)
    gate = jax.nn.sigmoid(project(flat, weights[4]))
    return (left.reshape(tokens, tokens, width), right.reshape(tokens, tokens, width), gate)

def finish(pair, summed, gate, gains, weight):
    width = pair.shape[2]
    flat = normalize(summed.reshape(-1, width), gains[1]).astype(jnp.bfloat16)
    result = pair.reshape(-1, width).astype(jnp.float32) + gate * project(flat, weight)
    return result.astype(jnp.bfloat16).reshape(pair.shape)

def reference(pair, tri_gains, tri_proj, tri_out, trans_gain, trans_up, trans_down):
    width = pair.shape[2]
    left, right, gate = prepare(pair, tri_gains[0], tri_proj[0])
    summed = jnp.einsum('ikc,jkc->ijc', left.astype(jnp.float32), right.astype(jnp.float32), precision=lax.Precision.HIGHEST)
    pair_mid = finish(pair, summed, gate, tri_gains[0], tri_out[0])
    left, right, gate = prepare(pair_mid, tri_gains[1], tri_proj[1])
    summed = jnp.einsum('kic,kjc->ijc', left.astype(jnp.float32), right.astype(jnp.float32), precision=lax.Precision.HIGHEST)
    pair_new = finish(pair_mid, summed, gate, tri_gains[1], tri_out[1])
    flat = normalize(pair_new.reshape(-1, width).astype(jnp.float32), trans_gain).astype(jnp.bfloat16)
    inner = (jax.nn.silu(project(flat, trans_up[0])) * project(flat, trans_up[1])).astype(jnp.bfloat16)
    result = pair_new.reshape(-1, width).astype(jnp.float32) + project(inner, trans_down)
    return result.astype(jnp.bfloat16).reshape(pair.shape)
```

```python
import functools

import jax
import jax.numpy as jnp
from jax import lax
from jax.experimental import pallas as pl
from jax.experimental.pallas import tpu as pltpu
from jax.sharding import PartitionSpec as P

GROUP = ("row", "col")


def normalize(values, gain):
    mean = jnp.mean(values, axis=-1, keepdims=True)
    centered = values - mean
    variance = jnp.mean(centered * centered, axis=-1, keepdims=True)
    return centered * lax.rsqrt(variance + 1e-05) * gain


def project(flat, weight):
    return jnp.dot(flat, weight, preferred_element_type=jnp.float32)


def exchange_kernel(n_row, n_col, x_ref, o_ref, send_sem, recv_sem, local_sem):
    n = n_row * n_col
    me = lax.axis_index("row") * n_col + lax.axis_index("col")

    def place(d):
        peer = lax.rem(me + d, n)
        return peer, {"row": peer // n_col, "col": lax.rem(peer, n_col)}

    barrier = pltpu.get_barrier_semaphore()

    def greet(d, _):
        pl.semaphore_signal(barrier, inc=1, device_id=place(d)[1], device_id_type=pl.DeviceIdType.MESH)
        return 0

    lax.fori_loop(1, n, greet, 0)
    own = pltpu.make_async_copy(x_ref.at[me], o_ref.at[me], local_sem)
    own.start()
    pl.semaphore_wait(barrier, n - 1)

    def send(d, _):
        peer, where = place(d)
        pltpu.make_async_remote_copy(
            src_ref=x_ref.at[peer], dst_ref=o_ref.at[me],
            send_sem=send_sem.at[d], recv_sem=recv_sem.at[d],
            device_id=where, device_id_type=pl.DeviceIdType.MESH,
        ).start()
        return 0

    lax.fori_loop(1, n, send, 0)

    def finish(d, _):
        peer, where = place(d)
        source = lax.rem(me - d + n, n)
        copy = pltpu.make_async_remote_copy(
            src_ref=x_ref.at[peer], dst_ref=o_ref.at[source],
            send_sem=send_sem.at[d], recv_sem=recv_sem.at[d],
            device_id=where, device_id_type=pl.DeviceIdType.MESH,
        )
        copy.wait_send()
        copy.wait_recv()
        return 0

    lax.fori_loop(1, n, finish, 0)
    own.wait()


def exchange(x, n_row, n_col, cid):
    n = n_row * n_col
    return pl.pallas_call(
        functools.partial(exchange_kernel, n_row, n_col),
        out_shape=jax.ShapeDtypeStruct(x.shape, x.dtype),
        in_specs=[pl.BlockSpec(memory_space=pltpu.VMEM)],
        out_specs=pl.BlockSpec(memory_space=pltpu.VMEM),
        scratch_shapes=[
            pltpu.SemaphoreType.DMA((n,)),
            pltpu.SemaphoreType.DMA((n,)),
            pltpu.SemaphoreType.DMA,
        ],
        compiler_params=pltpu.CompilerParams(
            collective_id=cid, has_side_effects=True, vmem_limit_bytes=40 * 1024 * 1024
        ),
        name=f"exchange_{cid}",
    )(x)


def pad_rows(x):
    short = -x.shape[1] % 16
    return jnp.pad(x, ((0, 0), (0, short), (0, 0))) if short else x


def on_device(n_row, n_col, pair, tri_gains, tri_proj, tri_out, trans_gain, trans_up, trans_down):
    rows, cols, width = pair.shape
    n = n_row * n_col
    cells = rows * cols
    each = width // n

    def update(pair, gains, weights, out_weight, spec, cid):
        flat = normalize(pair.reshape(-1, width).astype(jnp.float32), gains[0]).astype(jnp.bfloat16)

        def turned(weight):
            return lax.dot_general(weight, flat, (((0,), (1,)), ((), ())), preferred_element_type=jnp.float32)

        left = (jax.nn.sigmoid(turned(weights[1])) * turned(weights[0])).astype(jnp.bfloat16)
        right = (jax.nn.sigmoid(turned(weights[3])) * turned(weights[2])).astype(jnp.bfloat16)
        gate = jax.nn.sigmoid(project(flat, weights[4]))
        both = jnp.concatenate([left.reshape(n, each, cells), right.reshape(n, each, cells)], axis=1)
        both = exchange(pad_rows(both), n_row, n_col, cid)[:, : 2 * each]
        both = both.reshape(n_row, n_col, 2, each, rows, cols)
        both = jnp.transpose(both, (2, 3, 0, 4, 1, 5)).reshape(2, each, n_row * rows, n_col * cols)
        summed = jnp.einsum(spec, both[0], both[1], preferred_element_type=jnp.float32).astype(jnp.bfloat16)
        summed = summed.reshape(each, n_row, rows, n_col, cols)
        summed = jnp.transpose(summed, (1, 3, 0, 2, 4)).reshape(n, 2 * each, cells // 2)
        summed = exchange(pad_rows(summed), n_row, n_col, cid + 1)[:, : 2 * each]
        summed = jnp.transpose(summed.reshape(width, cells), (1, 0)).astype(jnp.float32)
        done = normalize(summed, gains[1]).astype(jnp.bfloat16)
        result = pair.reshape(-1, width).astype(jnp.float32) + gate * project(done, out_weight)
        return result.astype(jnp.bfloat16).reshape(pair.shape)

    pair_mid = update(pair, tri_gains[0], tri_proj[0], tri_out[0], "cik,cjk->cij", 0)
    pair_new = update(pair_mid, tri_gains[1], tri_proj[1], tri_out[1], "cki,ckj->cij", 2)
    flat = normalize(pair_new.reshape(-1, width).astype(jnp.float32), trans_gain).astype(jnp.bfloat16)
    inner = (jax.nn.silu(project(flat, trans_up[0])) * project(flat, trans_up[1])).astype(jnp.bfloat16)
    result = pair_new.reshape(-1, width).astype(jnp.float32) + project(inner, trans_down)
    return result.astype(jnp.bfloat16).reshape(rows, cols, width)


def solution(mesh):
    placed = (P(("rep", "row"), "col", None), P(), P(), P(), P(), P(), P())
    return jax.shard_map(
        functools.partial(on_device, mesh.shape["row"], mesh.shape["col"]),
        mesh=mesh,
        in_specs=placed,
        out_specs=P(("rep", "row"), "col", None),
        check_vma=False,
    )
```

```python
import functools

import jax
import jax.numpy as jnp
from jax import lax
from jax.experimental import pallas as pl
from jax.experimental.pallas import tpu as pltpu
from jax.sharding import PartitionSpec as P

GROUP = ("row", "col")


def normalize(values, gain):
    mean = jnp.mean(values, axis=-1, keepdims=True)
    centered = values - mean
    variance = jnp.mean(centered * centered, axis=-1, keepdims=True)
    return centered * lax.rsqrt(variance + 1e-05) * gain


def project(flat, weight):
    return jnp.dot(flat, weight, preferred_element_type=jnp.float32)


def exchange_kernel(n_row, n_col, x_ref, o_ref, send_sem, recv_sem, local_sem):
    n = n_row * n_col
    me = lax.axis_index("row") * n_col + lax.axis_index("col")

    def place(d):
        peer = lax.rem(me + d, n)
        return peer, {"row": peer // n_col, "col": lax.rem(peer, n_col)}

    barrier = pltpu.get_barrier_semaphore()

    def greet(d, _):
        pl.semaphore_signal(barrier, inc=1, device_id=place(d)[1], device_id_type=pl.DeviceIdType.MESH)
        return 0

    lax.fori_loop(1, n, greet, 0)
    own = pltpu.make_async_copy(x_ref.at[me], o_ref.at[me], local_sem)
    own.start()
    pl.semaphore_wait(barrier, n - 1)

    def send(d, _):
        peer, where = place(d)
        pltpu.make_async_remote_copy(
            src_ref=x_ref.at[peer], dst_ref=o_ref.at[me],
            send_sem=send_sem.at[d], recv_sem=recv_sem.at[d],
            device_id=where, device_id_type=pl.DeviceIdType.MESH,
        ).start()
        return 0

    lax.fori_loop(1, n, send, 0)

    def finish(d, _):
        peer, where = place(d)
        source = lax.rem(me - d + n, n)
        copy = pltpu.make_async_remote_copy(
            src_ref=x_ref.at[peer], dst_ref=o_ref.at[source],
            send_sem=send_sem.at[d], recv_sem=recv_sem.at[d],
            device_id=where, device_id_type=pl.DeviceIdType.MESH,
        )
        copy.wait_send()
        copy.wait_recv()
        return 0

    lax.fori_loop(1, n, finish, 0)
    own.wait()


def exchange(x, n_row, n_col, cid):
    n = n_row * n_col
    return pl.pallas_call(
        functools.partial(exchange_kernel, n_row, n_col),
        out_shape=jax.ShapeDtypeStruct(x.shape, x.dtype),
        in_specs=[pl.BlockSpec(memory_space=pltpu.VMEM)],
        out_specs=pl.BlockSpec(memory_space=pltpu.VMEM),
        scratch_shapes=[
            pltpu.SemaphoreType.DMA((n,)),
            pltpu.SemaphoreType.DMA((n,)),
            pltpu.SemaphoreType.DMA,
        ],
        compiler_params=pltpu.CompilerParams(
            collective_id=cid, has_side_effects=True, vmem_limit_bytes=40 * 1024 * 1024
        ),
        name=f"exchange_{cid}",
    )(x)


NT = (((1,), (1,)), ((), ()))
STEP = 896


def fused_kernel(
    n_row, n_col, rows, cols,
    x_ref, gains_ref, proj_ref, out_w_ref, tgain_ref, up_ref, down_ref, o_ref,
    turned, gate, mid, summed, lefts, rights, outs,
    send_a, recv_a, send_b, recv_b, send_c, recv_c, send_d, recv_d,
    ssem_a, rsem_a, ssem_b, rsem_b, ssem_c, rsem_c, ssem_d, rsem_d, local_sem,
):
    n = n_row * n_col
    cells = rows * cols
    each = 8
    all_rows = n_row * rows
    half = cells // 2
    half_rows = rows // 2
    back_tiles = recv_b.shape[2] // 128
    row = lax.axis_index("row")
    col = lax.axis_index("col")
    me = row * n_col + col
    f32, bf16 = jnp.float32, jnp.bfloat16
    starts = list(range(0, cells, STEP))
    padded = send_a.shape[2]
    lane = lax.broadcasted_iota(jnp.int32, (8, 128), 1)

    def place(d):
        peer = lax.rem(me + d, n)
        return peer, {"row": peer // n_col, "col": lax.rem(peer, n_col)}

    barrier = pltpu.get_barrier_semaphore()

    def greet(d, _):
        pl.semaphore_signal(barrier, inc=1, device_id=place(d)[1], device_id_type=pl.DeviceIdType.MESH)
        return 0

    lax.fori_loop(1, n, greet, 0)

    for u in range(2):
        for m in range(4):
            turned[u, m * 128 : (m + 1) * 128, :] = proj_ref[u, m].astype(f32).T.astype(bf16)
    tail = cells - cells // 128 * 128
    if tail:
        zero = jnp.zeros((n, 16, 128), bf16)
        send_a[:, :, padded - 128 :] = zero
        send_c[:, :, padded - 128 :] = zero

    def remote(send, recv, ssem, rsem, k, lo, size, d, source):
        peer, where = place(d)
        return pltpu.make_async_remote_copy(
            src_ref=send.at[peer, :, pl.ds(lo, size)],
            dst_ref=recv.at[source, :, pl.ds(lo, size)],
            send_sem=ssem.at[k, d], recv_sem=rsem.at[k, d],
            device_id=where, device_id_type=pl.DeviceIdType.MESH,
        )

    def span(k):
        lo = starts[k]
        return lo, (padded if k == len(starts) - 1 else lo + STEP) - lo

    def prepare(u, values, lo, size, send):
        flat = normalize(values, gains_ref[2 * u : 2 * u + 1, :]).astype(bf16)
        gate[lo : lo + size, :] = jax.nn.sigmoid(project(flat, proj_ref[u, 4]))
        for side in range(2):
            value = lax.dot_general(
                turned[u, 256 * side : 256 * side + 128, :], flat, NT, preferred_element_type=f32
            )
            scale = lax.dot_general(
                turned[u, 256 * side + 128 : 256 * side + 256, :], flat, NT, preferred_element_type=f32
            )
            held = (jax.nn.sigmoid(scale) * value).astype(bf16)
            send[:, each * side : each * side + each, lo : lo + size] = held.reshape(n, each, size)

    def send_chunk(k, send, recv, ssem, rsem):
        lo, size = span(k)

        def one(d, _):
            remote(send, recv, ssem, rsem, k, lo, size, d, me).start()
            return 0

        lax.fori_loop(1, n, one, 0)

    def shifted(tiles, start):
        t, s = start // 128, start % 128
        if s == 0:
            return tiles[t]
        first = pltpu.roll(tiles[t], 128 - s, 1)
        if s + cols <= 128:
            return first
        return jnp.where(lane < 128 - s, first, pltpu.roll(tiles[t + 1], 128 - s, 1))

    def unpack(recv, source):
        r, q = source // n_col, lax.rem(source, n_col)
        base = q * (each * all_rows) + r * rows
        tiles = [recv[source, :, 128 * t : 128 * t + 128].astype(f32) for t in range(padded // 128)]
        for side, held in ((0, lefts), (1, rights)):
            mine = [t[each * side : each * side + each] for t in tiles]
            for i in range(rows):
                value = jnp.where(lane < cols, shifted(mine, cols * i), 0.0)
                held[pl.ds(base + i, each, stride=all_rows), :] = value

    def receive(send, recv, ssem, rsem):
        own = pltpu.make_async_copy(send.at[me], recv.at[me], local_sem)
        own.start()
        own.wait()
        unpack(recv, me)

        def one(d, _):
            source = lax.rem(me - d + n, n)
            for k in range(len(starts)):
                lo, size = span(k)
                remote(send, recv, ssem, rsem, k, lo, size, d, source).wait_recv()
            unpack(recv, source)
            return 0

        lax.fori_loop(1, n, one, 0)

    def channel(held, q, c, offset, size):
        at = pl.multiple_of(q * (each * all_rows) + c * all_rows + offset, 8)
        return held[pl.ds(at, size), :]

    def outgoing(c, _):
        left = [channel(lefts, q, c, 0, all_rows).astype(bf16) for q in range(n_col)]
        for jq in range(n_col):
            total = None
            for q in range(n_col):
                right = channel(rights, q, c, jq * cols, 128).astype(bf16)
                term = lax.dot_general(left[q], right, NT, preferred_element_type=f32)
                total = term if total is None else total + term
            outs[pl.ds(jq * (each * all_rows) + c, all_rows, stride=each), :] = total
        return 0

    def incoming(c, _):
        right = [channel(rights, q, c, 0, all_rows).astype(bf16) for q in range(n_col)]
        for iq in range(n_col):
            left = channel(lefts, iq, c, 0, all_rows).T.astype(bf16)
            for jq in range(n_col):
                total = project(left, right[jq])[:cols]
                at = jq * (each * all_rows) + iq * cols * each + c
                outs[pl.ds(at, cols, stride=each), :] = total
        return 0

    def pack(send, dest):
        r, q = dest // n_col, lax.rem(dest, n_col)
        base = q * (each * all_rows) + r * rows * each
        for t in range(back_tiles):
            parts = []
            for h in range(2):
                total = jnp.zeros((8, 128), f32)
                for i in range(half_rows):
                    at = i * cols - 128 * t
                    if at >= 128 or at + cols <= 0:
                        continue
                    spot = pl.multiple_of(base + (h * half_rows + i) * each, 8)
                    value = outs[pl.ds(spot, each), :]
                    if at % 128:
                        value = pltpu.roll(value, at % 128, 1)
                    total = jnp.where((lane >= at) & (lane < at + cols), value, total)
                parts.append(total)
            send[dest, :, 128 * t : 128 * t + 128] = jnp.concatenate(parts, axis=0).astype(bf16)

    def give_back(send, recv, ssem, rsem):
        width = send.shape[2]

        def one(d, _):
            pack(send, place(d)[0])
            remote(send, recv, ssem, rsem, 0, 0, width, d, me).start()
            return 0

        lax.fori_loop(1, n, one, 0)
        pack(send, me)
        own = pltpu.make_async_copy(send.at[me], recv.at[me], local_sem)
        own.start()
        own.wait()

        def done(d, _):
            remote(send, recv, ssem, rsem, 0, 0, width, d, lax.rem(me - d + n, n)).wait_recv()
            return 0

        lax.fori_loop(1, n, done, 0)
        for t in range(back_tiles):
            tile = recv[:, :, 128 * t : 128 * t + 128].astype(f32)
            keep = min(128, half - 128 * t)
            for h in range(2):
                piece = tile[:, each * h : each * h + each, :].reshape(n * each, 128).T
                summed[h * half + 128 * t : h * half + 128 * t + keep, :] = piece[:keep]

    def finish(u, before, lo, size):
        done = normalize(summed[pl.ds(lo, size), :], gains_ref[2 * u + 1 : 2 * u + 2, :]).astype(bf16)
        result = before.astype(f32) + gate[pl.ds(lo, size), :] * project(done, out_w_ref[u])
        return result.astype(bf16)

    for k, lo in enumerate(starts):
        size = min(STEP, cells - lo)
        prepare(0, x_ref[lo : lo + size, :].astype(f32), lo, size, send_a)
        if k == 0:
            pl.semaphore_wait(barrier, n - 1)
        send_chunk(k, send_a, recv_a, ssem_a, rsem_a)
    receive(send_a, recv_a, ssem_a, rsem_a)
    lax.fori_loop(0, each, outgoing, 0)
    give_back(send_b, recv_b, ssem_b, rsem_b)
    for k, lo in enumerate(starts):
        size = min(STEP, cells - lo)
        held = finish(0, x_ref[lo : lo + size, :], lo, size)
        mid[lo : lo + size, :] = held
        prepare(1, held.astype(f32), lo, size, send_c)
        send_chunk(k, send_c, recv_c, ssem_c, rsem_c)
    receive(send_c, recv_c, ssem_c, rsem_c)
    lax.fori_loop(0, each, incoming, 0)
    give_back(send_d, recv_d, ssem_d, rsem_d)

    last = STEP // 2

    def transition(k, _):
        lo = pl.multiple_of(k * last, 16)
        new = finish(1, mid[pl.ds(lo, last), :], lo, last).astype(f32)
        flat = normalize(new, tgain_ref[...]).astype(bf16)
        first = project(flat, up_ref[0])
        inner = (first * jax.nn.sigmoid(first) * project(flat, up_ref[1])).astype(bf16)
        o_ref[pl.ds(lo, last), :] = (new + project(inner, down_ref[...])).astype(bf16)
        return 0

    lax.fori_loop(0, cells // last, transition, 0)

    def drain(d, _):
        for send, recv, ssem, rsem in ((send_a, recv_a, ssem_a, rsem_a), (send_c, recv_c, ssem_c, rsem_c)):
            for k in range(len(starts)):
                lo, size = span(k)
                remote(send, recv, ssem, rsem, k, lo, size, d, me).wait_send()
        for send, recv, ssem, rsem in ((send_b, recv_b, ssem_b, rsem_b), (send_d, recv_d, ssem_d, rsem_d)):
            remote(send, recv, ssem, rsem, 0, 0, send.shape[2], d, me).wait_send()
        return 0

    lax.fori_loop(1, n, drain, 0)


def fused(n_row, n_col, pair, tri_gains, tri_proj, tri_out, trans_gain, trans_up, trans_down):
    rows, cols, width = pair.shape
    n = n_row * n_col
    cells = rows * cols
    up128 = lambda v: -(-v // 128) * 128
    ahead = pltpu.VMEM((n, 16, up128(cells)), jnp.bfloat16)
    back = pltpu.VMEM((n, 16, up128(cells // 2)), jnp.bfloat16)
    chunks = -(-cells // STEP)
    panel = pltpu.VMEM((n_col * 8 * n_row * rows + 16, 128), jnp.float32)
    many = pltpu.SemaphoreType.DMA((chunks, n))
    few = pltpu.SemaphoreType.DMA((1, n))
    whole = pl.BlockSpec(memory_space=pltpu.VMEM)
    out = pl.pallas_call(
        functools.partial(fused_kernel, n_row, n_col, rows, cols),
        out_shape=jax.ShapeDtypeStruct((cells, width), pair.dtype),
        in_specs=[whole] * 7,
        out_specs=whole,
        scratch_shapes=[
            pltpu.VMEM((2, 4 * width, width), jnp.bfloat16),
            pltpu.VMEM((cells, width), jnp.float32),
            pltpu.VMEM((cells, width), jnp.bfloat16),
            pltpu.VMEM((cells, width), jnp.float32),
            panel, panel, panel,
            ahead, ahead, back, back, ahead, ahead, back, back,
            many, many, few, few, many, many, few, few,
            pltpu.SemaphoreType.DMA,
        ],
        compiler_params=pltpu.CompilerParams(
            collective_id=4, has_side_effects=True, vmem_limit_bytes=56 * 1024 * 1024
        ),
        name="fused",
    )(
        pair.reshape(cells, width), tri_gains.reshape(4, width), tri_proj, tri_out,
        trans_gain.reshape(1, width), trans_up, trans_down,
    )
    return out.reshape(rows, cols, width)


def pad_rows(x):
    short = -x.shape[1] % 16
    return jnp.pad(x, ((0, 0), (0, short), (0, 0))) if short else x


def on_device(n_row, n_col, pair, tri_gains, tri_proj, tri_out, trans_gain, trans_up, trans_down):
    rows, cols, width = pair.shape
    n = n_row * n_col
    cells = rows * cols
    each = width // n
    if each == 8 and width == 128 and n_row * rows == n_col * cols and cols % 16 == 0 and cells % (STEP // 2) == 0:
        return fused(n_row, n_col, pair, tri_gains, tri_proj, tri_out, trans_gain, trans_up, trans_down)

    def update(pair, gains, weights, out_weight, spec, cid):
        flat = normalize(pair.reshape(-1, width).astype(jnp.float32), gains[0]).astype(jnp.bfloat16)

        def turned(weight):
            return lax.dot_general(weight, flat, (((0,), (1,)), ((), ())), preferred_element_type=jnp.float32)

        left = (jax.nn.sigmoid(turned(weights[1])) * turned(weights[0])).astype(jnp.bfloat16)
        right = (jax.nn.sigmoid(turned(weights[3])) * turned(weights[2])).astype(jnp.bfloat16)
        gate = jax.nn.sigmoid(project(flat, weights[4]))
        both = jnp.concatenate([left.reshape(n, each, cells), right.reshape(n, each, cells)], axis=1)
        both = exchange(pad_rows(both), n_row, n_col, cid)[:, : 2 * each]
        both = both.reshape(n_row, n_col, 2, each, rows, cols)
        both = jnp.transpose(both, (2, 3, 0, 4, 1, 5)).reshape(2, each, n_row * rows, n_col * cols)
        summed = jnp.einsum(spec, both[0], both[1], preferred_element_type=jnp.float32).astype(jnp.bfloat16)
        summed = summed.reshape(each, n_row, rows, n_col, cols)
        summed = jnp.transpose(summed, (1, 3, 0, 2, 4)).reshape(n, 2 * each, cells // 2)
        summed = exchange(pad_rows(summed), n_row, n_col, cid + 1)[:, : 2 * each]
        summed = jnp.transpose(summed.reshape(width, cells), (1, 0)).astype(jnp.float32)
        done = normalize(summed, gains[1]).astype(jnp.bfloat16)
        result = pair.reshape(-1, width).astype(jnp.float32) + gate * project(done, out_weight)
        return result.astype(jnp.bfloat16).reshape(pair.shape)

    pair_mid = update(pair, tri_gains[0], tri_proj[0], tri_out[0], "cik,cjk->cij", 0)
    pair_new = update(pair_mid, tri_gains[1], tri_proj[1], tri_out[1], "cki,ckj->cij", 2)
    flat = normalize(pair_new.reshape(-1, width).astype(jnp.float32), trans_gain).astype(jnp.bfloat16)
    inner = (jax.nn.silu(project(flat, trans_up[0])) * project(flat, trans_up[1])).astype(jnp.bfloat16)
    result = pair_new.reshape(-1, width).astype(jnp.float32) + project(inner, trans_down)
    return result.astype(jnp.bfloat16).reshape(rows, cols, width)


def solution(mesh):
    placed = (P(("rep", "row"), "col", None), P(), P(), P(), P(), P(), P())
    return jax.shard_map(
        functools.partial(on_device, mesh.shape["row"], mesh.shape["col"]),
        mesh=mesh,
        in_specs=placed,
        out_specs=P(("rep", "row"), "col", None),
        check_vma=False,
    )
```

```python
import functools

import jax
import jax.numpy as jnp
from jax import lax
from jax.experimental import pallas as pl
from jax.experimental.pallas import tpu as pltpu
from jax.sharding import PartitionSpec as P

GROUP = ("row", "col")


def normalize(values, gain):
    mean = jnp.mean(values, axis=-1, keepdims=True)
    centered = values - mean
    variance = jnp.mean(centered * centered, axis=-1, keepdims=True)
    return centered * lax.rsqrt(variance + 1e-05) * gain


def project(flat, weight):
    return jnp.dot(flat, weight, preferred_element_type=jnp.float32)


def exchange_kernel(n_row, n_col, x_ref, o_ref, send_sem, recv_sem, local_sem):
    n = n_row * n_col
    me = lax.axis_index("row") * n_col + lax.axis_index("col")

    def place(d):
        peer = lax.rem(me + d, n)
        return peer, {"row": peer // n_col, "col": lax.rem(peer, n_col)}

    barrier = pltpu.get_barrier_semaphore()

    def greet(d, _):
        pl.semaphore_signal(barrier, inc=1, device_id=place(d)[1], device_id_type=pl.DeviceIdType.MESH)
        return 0

    lax.fori_loop(1, n, greet, 0)
    own = pltpu.make_async_copy(x_ref.at[me], o_ref.at[me], local_sem)
    own.start()
    pl.semaphore_wait(barrier, n - 1)

    def send(d, _):
        peer, where = place(d)
        pltpu.make_async_remote_copy(
            src_ref=x_ref.at[peer], dst_ref=o_ref.at[me],
            send_sem=send_sem.at[d], recv_sem=recv_sem.at[d],
            device_id=where, device_id_type=pl.DeviceIdType.MESH,
        ).start()
        return 0

    lax.fori_loop(1, n, send, 0)

    def finish(d, _):
        peer, where = place(d)
        source = lax.rem(me - d + n, n)
        copy = pltpu.make_async_remote_copy(
            src_ref=x_ref.at[peer], dst_ref=o_ref.at[source],
            send_sem=send_sem.at[d], recv_sem=recv_sem.at[d],
            device_id=where, device_id_type=pl.DeviceIdType.MESH,
        )
        copy.wait_send()
        copy.wait_recv()
        return 0

    lax.fori_loop(1, n, finish, 0)
    own.wait()


def exchange(x, n_row, n_col, cid):
    n = n_row * n_col
    return pl.pallas_call(
        functools.partial(exchange_kernel, n_row, n_col),
        out_shape=jax.ShapeDtypeStruct(x.shape, x.dtype),
        in_specs=[pl.BlockSpec(memory_space=pltpu.VMEM)],
        out_specs=pl.BlockSpec(memory_space=pltpu.VMEM),
        scratch_shapes=[
            pltpu.SemaphoreType.DMA((n,)),
            pltpu.SemaphoreType.DMA((n,)),
            pltpu.SemaphoreType.DMA,
        ],
        compiler_params=pltpu.CompilerParams(
            collective_id=cid, has_side_effects=True, vmem_limit_bytes=40 * 1024 * 1024
        ),
        name=f"exchange_{cid}",
    )(x)


NT = (((1,), (1,)), ((), ()))
TALL = 8


def fused_kernel(
    n_row, n_col, rows, cols,
    x_ref, gains_ref, proj_ref, out_w_ref, tgain_ref, up_ref, down_ref, o_ref,
    turned, gate, mid, summed, lefts, rights, outs,
    send_a, recv_a, send_b, recv_b, send_c, recv_c, send_d, recv_d,
    ssem_a, rsem_a, ssem_b, rsem_b, ssem_c, rsem_c, ssem_d, rsem_d,
):
    n = n_row * n_col
    cells = rows * cols
    each = 8
    all_rows = n_row * rows
    step = TALL * cols
    h = n // 2
    row = lax.axis_index("row")
    col = lax.axis_index("col")
    me = row * n_col + col
    f32, bf16 = jnp.float32, jnp.bfloat16
    starts = list(range(0, cells, step))
    padded = send_a.shape[2]
    lane = lax.broadcasted_iota(jnp.int32, (8, 128), 1)

    def place(s):
        side = lax.rem(me // h + 1 + s // h, 2)
        peer = side * h + lax.rem(lax.rem(me, h) + s, h)
        source = side * h + lax.rem(lax.rem(me, h) + n - s, h)
        return peer, source, {"row": peer // n_col, "col": lax.rem(peer, n_col)}

    def peers(body):
        def one(s, _):
            body(s)
            return 0

        lax.fori_loop(0, h, one, 0)
        lax.fori_loop(h + 1, n, one, 0)

    barrier = pltpu.get_barrier_semaphore()

    def greet(s):
        pl.semaphore_signal(barrier, inc=1, device_id=place(s)[2], device_id_type=pl.DeviceIdType.MESH)

    peers(greet)

    for u in range(2):
        for m in range(4):
            turned[u, m * 128 : (m + 1) * 128, :] = proj_ref[u, m].astype(f32).T.astype(bf16)
    tail = cells - cells // 128 * 128
    if tail:
        zero = jnp.zeros((n, 16, 128), bf16)
        send_a[:, :, padded - 128 :] = zero
        send_c[:, :, padded - 128 :] = zero

    def remote(send, recv, ssem, rsem, k, lo, size, s, arriving):
        peer, source, where = place(s)
        return pltpu.make_async_remote_copy(
            src_ref=send.at[peer, :, pl.ds(lo, size)],
            dst_ref=recv.at[source if arriving else me, :, pl.ds(lo, size)],
            send_sem=ssem.at[k, s], recv_sem=rsem.at[k, s],
            device_id=where, device_id_type=pl.DeviceIdType.MESH,
        )

    def span(k):
        lo = starts[k]
        return lo, (padded if k == len(starts) - 1 else lo + step) - lo

    def prepare(u, values, lo, size, send):
        flat = normalize(values, gains_ref[2 * u : 2 * u + 1, :]).astype(bf16)
        gate[lo : lo + size, :] = jax.nn.sigmoid(project(flat, proj_ref[u, 4]))
        for side in range(2):
            value = lax.dot_general(
                turned[u, 256 * side : 256 * side + 128, :], flat, NT, preferred_element_type=f32
            )
            scale = lax.dot_general(
                turned[u, 256 * side + 128 : 256 * side + 256, :], flat, NT, preferred_element_type=f32
            )
            held = (jax.nn.sigmoid(scale) * value).astype(bf16)
            send[:, each * side : each * side + each, lo : lo + size] = held.reshape(n, each, size)

    def send_chunk(k, send, recv, ssem, rsem):
        lo, size = span(k)
        peers(lambda s: remote(send, recv, ssem, rsem, k, lo, size, s, False).start())
        unpack(send, me, k)

    def shifted(tiles, start):
        t, s = start // 128, start % 128
        if s == 0:
            return tiles[t]
        first = pltpu.roll(tiles[t], 128 - s, 1)
        if s + cols <= 128:
            return first
        return jnp.where(lane < 128 - s, first, pltpu.roll(tiles[t + 1], 128 - s, 1))

    def unpack(ref, source, k):
        lo, size = span(k)
        r, q = source // n_col, lax.rem(source, n_col)
        base = q * (each * all_rows) + r * rows
        tiles = [ref[source, :, lo + at : lo + at + 128].astype(f32) for at in range(0, size, 128)]
        for side, held in ((0, lefts), (1, rights)):
            mine = [t[each * side : each * side + each] for t in tiles]
            for i in range(min(TALL, rows - TALL * k)):
                value = jnp.where(lane < cols, shifted(mine, cols * i), 0.0)
                held[pl.ds(base + TALL * k + i, each, stride=all_rows), :] = value

    def receive(order, send, recv, ssem, rsem):
        for k in order:
            lo, size = span(k)

            def one(s):
                remote(send, recv, ssem, rsem, k, lo, size, s, True).wait_recv()
                unpack(recv, place(s)[1], k)

            peers(one)

    def channel(held, q, c, offset, size):
        at = pl.multiple_of(q * (each * all_rows) + c * all_rows + offset, 8)
        return held[pl.ds(at, size), :]

    def outgoing(c, _):
        left = [channel(lefts, q, c, 0, all_rows).astype(bf16) for q in range(n_col)]
        for jq in range(n_col):
            total = None
            for q in range(n_col):
                right = channel(rights, q, c, jq * cols, 128).astype(bf16)
                term = lax.dot_general(left[q], right, NT, preferred_element_type=f32)
                total = term if total is None else total + term
            outs[pl.ds(jq * (each * all_rows) + c, all_rows, stride=each), :] = total
        return 0

    def incoming(c, _):
        right = [channel(rights, q, c, 0, all_rows).astype(bf16) for q in range(n_col)]
        for iq in range(n_col):
            left = channel(lefts, iq, c, 0, all_rows).T.astype(bf16)
            for jq in range(n_col):
                total = project(left, right[jq])[:cols]
                at = jq * (each * all_rows) + iq * cols * each + c
                outs[pl.ds(at, cols, stride=each), :] = total
        return 0

    def pack(ref, dest, g):
        r, q = dest // n_col, lax.rem(dest, n_col)
        base = q * (each * all_rows) + r * rows * each
        for t in range(step // 128):
            parts = []
            for k in (g, g + 2):
                total = jnp.zeros((8, 128), f32)
                for i in range(min(TALL, rows - TALL * k)):
                    at = i * cols - 128 * t
                    if at >= 128 or at + cols <= 0:
                        continue
                    spot = pl.multiple_of(base + (TALL * k + i) * each, 8)
                    value = outs[pl.ds(spot, each), :]
                    if at % 128:
                        value = pltpu.roll(value, at % 128, 1)
                    total = jnp.where((lane >= at) & (lane < at + cols), value, total)
                parts.append(total)
            lo = g * step + 128 * t
            ref[dest, :, lo : lo + 128] = jnp.concatenate(parts, axis=0).astype(bf16)

    def give_back(send, recv, ssem, rsem):
        for g in range(2):

            def one(s):
                pack(send, place(s)[0], g)
                remote(send, recv, ssem, rsem, g, g * step, step, s, False).start()

            peers(one)
        for g in range(2):
            pack(recv, me, g)

    def take_back(g, send, recv, ssem, rsem):
        peers(lambda s: remote(send, recv, ssem, rsem, g, g * step, step, s, True).wait_recv())
        for t in range(step // 128):
            lo = g * step + 128 * t
            tile = recv[:, :, lo : lo + 128].astype(f32)
            for half in range(2):
                at = (g + 2 * half) * step + 128 * t
                keep = min(128, cells - at)
                if keep > 0:
                    piece = tile[:, each * half : each * half + each, :].reshape(n * each, 128).T
                    summed[at : at + keep, :] = piece[:keep]

    def finish(u, before, lo, size):
        done = normalize(summed[pl.ds(lo, size), :], gains_ref[2 * u + 1 : 2 * u + 2, :]).astype(bf16)
        result = before.astype(f32) + gate[pl.ds(lo, size), :] * project(done, out_w_ref[u])
        return result.astype(bf16)

    def bounds(k):
        return starts[k], min(step, cells - starts[k])

    ahead_a = (send_a, recv_a, ssem_a, rsem_a)
    back_a = (send_b, recv_b, ssem_b, rsem_b)
    ahead_b = (send_c, recv_c, ssem_c, rsem_c)
    back_b = (send_d, recv_d, ssem_d, rsem_d)
    for k in range(4):
        lo, size = bounds(k)
        prepare(0, x_ref[lo : lo + size, :].astype(f32), lo, size, send_a)
        if k == 0:
            pl.semaphore_wait(barrier, n - 1)
        send_chunk(k, *ahead_a)
    receive((0, 1, 2, 3), *ahead_a)
    lax.fori_loop(0, each, outgoing, 0)
    give_back(*back_a)
    for g in range(2):
        take_back(g, *back_a)
        for k in (g, g + 2):
            lo, size = bounds(k)
            held = finish(0, x_ref[lo : lo + size, :], lo, size)
            mid[lo : lo + size, :] = held
            prepare(1, held.astype(f32), lo, size, send_c)
            send_chunk(k, *ahead_b)
    receive((0, 2, 1, 3), *ahead_b)
    lax.fori_loop(0, each, incoming, 0)
    give_back(*back_b)

    last = step // 2

    def transition(k, _):
        lo = pl.multiple_of(k * last, 16)
        new = finish(1, mid[pl.ds(lo, last), :], lo, last).astype(f32)
        flat = normalize(new, tgain_ref[...]).astype(bf16)
        first = project(flat, up_ref[0])
        inner = (first * jax.nn.sigmoid(first) * project(flat, up_ref[1])).astype(bf16)
        o_ref[pl.ds(lo, last), :] = (new + project(inner, down_ref[...])).astype(bf16)
        return 0

    for g in range(2):
        take_back(g, *back_b)
        for k in (g, g + 2):
            lo, size = bounds(k)
            lax.fori_loop(lo // last, (lo + size) // last, transition, 0)

    def drain(s):
        for held in (ahead_a, ahead_b):
            for k in range(4):
                lo, size = span(k)
                remote(*held, k, lo, size, s, True).wait_send()
        for held in (back_a, back_b):
            for g in range(2):
                remote(*held, g, g * step, step, s, True).wait_send()

    peers(drain)


def fused(n_row, n_col, pair, tri_gains, tri_proj, tri_out, trans_gain, trans_up, trans_down):
    rows, cols, width = pair.shape
    n = n_row * n_col
    cells = rows * cols
    up128 = lambda v: -(-v // 128) * 128
    ahead = pltpu.VMEM((n, 16, up128(cells)), jnp.bfloat16)
    back = pltpu.VMEM((n, 16, 2 * TALL * cols), jnp.bfloat16)
    panel = pltpu.VMEM((n_col * 8 * n_row * rows + 16, 128), jnp.float32)
    many = pltpu.SemaphoreType.DMA((4, n))
    few = pltpu.SemaphoreType.DMA((2, n))
    whole = pl.BlockSpec(memory_space=pltpu.VMEM)
    out = pl.pallas_call(
        functools.partial(fused_kernel, n_row, n_col, rows, cols),
        out_shape=jax.ShapeDtypeStruct((cells, width), pair.dtype),
        in_specs=[whole] * 7,
        out_specs=whole,
        scratch_shapes=[
            pltpu.VMEM((2, 4 * width, width), jnp.bfloat16),
            pltpu.VMEM((cells, width), jnp.float32),
            pltpu.VMEM((cells, width), jnp.bfloat16),
            pltpu.VMEM((cells, width), jnp.float32),
            panel, panel, panel,
            ahead, ahead, back, back, ahead, ahead, back, back,
            many, many, few, few, many, many, few, few,
        ],
        compiler_params=pltpu.CompilerParams(
            collective_id=4, has_side_effects=True, vmem_limit_bytes=56 * 1024 * 1024
        ),
        name="fused",
    )(
        pair.reshape(cells, width), tri_gains.reshape(4, width), tri_proj, tri_out,
        trans_gain.reshape(1, width), trans_up, trans_down,
    )
    return out.reshape(rows, cols, width)


def pad_rows(x):
    short = -x.shape[1] % 16
    return jnp.pad(x, ((0, 0), (0, short), (0, 0))) if short else x


def on_device(n_row, n_col, pair, tri_gains, tri_proj, tri_out, trans_gain, trans_up, trans_down):
    rows, cols, width = pair.shape
    n = n_row * n_col
    cells = rows * cols
    each = width // n
    square = n_row * rows == n_col * cols
    if each == 8 and width == 128 and square and n % 2 == 0 and cols % 16 == 0 and rows in (28, 32):
        return fused(n_row, n_col, pair, tri_gains, tri_proj, tri_out, trans_gain, trans_up, trans_down)

    def update(pair, gains, weights, out_weight, spec, cid):
        flat = normalize(pair.reshape(-1, width).astype(jnp.float32), gains[0]).astype(jnp.bfloat16)

        def turned(weight):
            return lax.dot_general(weight, flat, (((0,), (1,)), ((), ())), preferred_element_type=jnp.float32)

        left = (jax.nn.sigmoid(turned(weights[1])) * turned(weights[0])).astype(jnp.bfloat16)
        right = (jax.nn.sigmoid(turned(weights[3])) * turned(weights[2])).astype(jnp.bfloat16)
        gate = jax.nn.sigmoid(project(flat, weights[4]))
        both = jnp.concatenate([left.reshape(n, each, cells), right.reshape(n, each, cells)], axis=1)
        both = exchange(pad_rows(both), n_row, n_col, cid)[:, : 2 * each]
        both = both.reshape(n_row, n_col, 2, each, rows, cols)
        both = jnp.transpose(both, (2, 3, 0, 4, 1, 5)).reshape(2, each, n_row * rows, n_col * cols)
        summed = jnp.einsum(spec, both[0], both[1], preferred_element_type=jnp.float32).astype(jnp.bfloat16)
        summed = summed.reshape(each, n_row, rows, n_col, cols)
        summed = jnp.transpose(summed, (1, 3, 0, 2, 4)).reshape(n, 2 * each, cells // 2)
        summed = exchange(pad_rows(summed), n_row, n_col, cid + 1)[:, : 2 * each]
        summed = jnp.transpose(summed.reshape(width, cells), (1, 0)).astype(jnp.float32)
        done = normalize(summed, gains[1]).astype(jnp.bfloat16)
        result = pair.reshape(-1, width).astype(jnp.float32) + gate * project(done, out_weight)
        return result.astype(jnp.bfloat16).reshape(pair.shape)

    pair_mid = update(pair, tri_gains[0], tri_proj[0], tri_out[0], "cik,cjk->cij", 0)
    pair_new = update(pair_mid, tri_gains[1], tri_proj[1], tri_out[1], "cki,ckj->cij", 2)
    flat = normalize(pair_new.reshape(-1, width).astype(jnp.float32), trans_gain).astype(jnp.bfloat16)
    inner = (jax.nn.silu(project(flat, trans_up[0])) * project(flat, trans_up[1])).astype(jnp.bfloat16)
    result = pair_new.reshape(-1, width).astype(jnp.float32) + project(inner, trans_down)
    return result.astype(jnp.bfloat16).reshape(rows, cols, width)


def solution(mesh):
    placed = (P(("rep", "row"), "col", None), P(), P(), P(), P(), P(), P())
    return jax.shard_map(
        functools.partial(on_device, mesh.shape["row"], mesh.shape["col"]),
        mesh=mesh,
        in_specs=placed,
        out_specs=P(("rep", "row"), "col", None),
        check_vma=False,
    )
```

```python
import functools

import jax
import jax.numpy as jnp
from jax import lax
from jax.experimental import pallas as pl
from jax.experimental.pallas import tpu as pltpu
from jax.sharding import PartitionSpec as P

GROUP = ("row", "col")


def normalize(values, gain):
    mean = jnp.mean(values, axis=-1, keepdims=True)
    centered = values - mean
    variance = jnp.mean(centered * centered, axis=-1, keepdims=True)
    return centered * lax.rsqrt(variance + 1e-05) * gain


def project(flat, weight):
    return jnp.dot(flat, weight, preferred_element_type=jnp.float32)


def exchange_kernel(n_row, n_col, x_ref, o_ref, send_sem, recv_sem, local_sem):
    n = n_row * n_col
    me = lax.axis_index("row") * n_col + lax.axis_index("col")

    def place(d):
        peer = lax.rem(me + d, n)
        return peer, {"row": peer // n_col, "col": lax.rem(peer, n_col)}

    barrier = pltpu.get_barrier_semaphore()

    def greet(d, _):
        pl.semaphore_signal(barrier, inc=1, device_id=place(d)[1], device_id_type=pl.DeviceIdType.MESH)
        return 0

    lax.fori_loop(1, n, greet, 0)
    own = pltpu.make_async_copy(x_ref.at[me], o_ref.at[me], local_sem)
    own.start()
    pl.semaphore_wait(barrier, n - 1)

    def send(d, _):
        peer, where = place(d)
        pltpu.make_async_remote_copy(
            src_ref=x_ref.at[peer], dst_ref=o_ref.at[me],
            send_sem=send_sem.at[d], recv_sem=recv_sem.at[d],
            device_id=where, device_id_type=pl.DeviceIdType.MESH,
        ).start()
        return 0

    lax.fori_loop(1, n, send, 0)

    def finish(d, _):
        peer, where = place(d)
        source = lax.rem(me - d + n, n)
        copy = pltpu.make_async_remote_copy(
            src_ref=x_ref.at[peer], dst_ref=o_ref.at[source],
            send_sem=send_sem.at[d], recv_sem=recv_sem.at[d],
            device_id=where, device_id_type=pl.DeviceIdType.MESH,
        )
        copy.wait_send()
        copy.wait_recv()
        return 0

    lax.fori_loop(1, n, finish, 0)
    own.wait()


def exchange(x, n_row, n_col, cid):
    n = n_row * n_col
    return pl.pallas_call(
        functools.partial(exchange_kernel, n_row, n_col),
        out_shape=jax.ShapeDtypeStruct(x.shape, x.dtype),
        in_specs=[pl.BlockSpec(memory_space=pltpu.VMEM)],
        out_specs=pl.BlockSpec(memory_space=pltpu.VMEM),
        scratch_shapes=[
            pltpu.SemaphoreType.DMA((n,)),
            pltpu.SemaphoreType.DMA((n,)),
            pltpu.SemaphoreType.DMA,
        ],
        compiler_params=pltpu.CompilerParams(
            collective_id=cid, has_side_effects=True, vmem_limit_bytes=40 * 1024 * 1024
        ),
        name=f"exchange_{cid}",
    )(x)


NT = (((1,), (1,)), ((), ()))
TALL = 8


def fused_kernel(
    n_row, n_col, rows, cols,
    x_ref, gains_ref, proj_ref, out_w_ref, tgain_ref, up_ref, down_ref, o_ref,
    turned, gate, mid, summed, lefts, rights, outs,
    send_l, recv_l, send_r, recv_r, send_b, recv_b, send_c, recv_c, send_d, recv_d,
    ssem_l, rsem_l, ssem_r, rsem_r, ssem_b, rsem_b, ssem_c, rsem_c, ssem_d, rsem_d,
):
    n = n_row * n_col
    cells = rows * cols
    each = 8
    all_rows = n_row * rows
    step = TALL * cols
    h = n // 2
    row = lax.axis_index("row")
    col = lax.axis_index("col")
    me = row * n_col + col
    f32, bf16 = jnp.float32, jnp.bfloat16
    starts = list(range(0, cells, step))
    padded = send_c.shape[2]
    wide = 2 * each
    some_rows = all_rows // 2
    lane_wide = lax.broadcasted_iota(jnp.int32, (16, 128), 1)
    lane = lax.broadcasted_iota(jnp.int32, (8, 128), 1)

    def place(s):
        side = lax.rem(me // h + 1 + s // h, 2)
        peer = side * h + lax.rem(lax.rem(me, h) + s, h)
        source = side * h + lax.rem(lax.rem(me, h) + n - s, h)
        return peer, source, {"row": peer // n_col, "col": lax.rem(peer, n_col)}

    def peers(body):
        def one(s, _):
            body(s)
            return 0

        lax.fori_loop(0, h, one, 0)
        lax.fori_loop(h + 1, n, one, 0)

    def near(body):
        def one(s, _):
            body(s)
            return 0

        lax.fori_loop(h + 1, n, one, 0)

    barrier = pltpu.get_barrier_semaphore()

    def greet(s):
        pl.semaphore_signal(barrier, inc=1, device_id=place(s)[2], device_id_type=pl.DeviceIdType.MESH)

    peers(greet)

    for u in range(2):
        for m in range(4):
            turned[u, m * 128 : (m + 1) * 128, :] = proj_ref[u, m].astype(f32).T.astype(bf16)
    tail = cells - cells // 128 * 128
    if tail:
        zero = jnp.zeros((n, 16, 128), bf16)
        send_l[:, :, padded - 128 :] = zero[:h]
        send_r[:, :, padded - 128 :] = zero[:h]
        send_c[:, :, padded - 128 :] = zero

    def remote(send, recv, ssem, rsem, k, lo, size, s, arriving):
        peer, source, where = place(s)
        return pltpu.make_async_remote_copy(
            src_ref=send.at[peer, :, pl.ds(lo, size)],
            dst_ref=recv.at[source if arriving else me, :, pl.ds(lo, size)],
            send_sem=ssem.at[k, s], recv_sem=rsem.at[k, s],
            device_id=where, device_id_type=pl.DeviceIdType.MESH,
        )

    def span(k):
        lo = starts[k]
        return lo, (padded if k == len(starts) - 1 else lo + step) - lo

    def prepare(u, values, lo, size, send):
        flat = normalize(values, gains_ref[2 * u : 2 * u + 1, :]).astype(bf16)
        gate[lo : lo + size, :] = jax.nn.sigmoid(project(flat, proj_ref[u, 4]))
        for side in range(2):
            value = lax.dot_general(
                turned[u, 256 * side : 256 * side + 128, :], flat, NT, preferred_element_type=f32
            )
            scale = lax.dot_general(
                turned[u, 256 * side + 128 : 256 * side + 256, :], flat, NT, preferred_element_type=f32
            )
            held = (jax.nn.sigmoid(scale) * value).astype(bf16)
            if u == 0:
                send[side][:, :, lo : lo + size] = held.reshape(h, wide, size)
            else:
                send[:, each * side : each * side + each, lo : lo + size] = held.reshape(n, each, size)

    def send_chunk(k, send, recv, ssem, rsem):
        lo, size = span(k)
        peers(lambda s: remote(send, recv, ssem, rsem, k, lo, size, s, False).start())
        unpack(send, me, k)

    def shifted(tiles, start):
        t, s = start // 128, start % 128
        if s == 0:
            return tiles[t]
        first = pltpu.roll(tiles[t], 128 - s, 1)
        if s + cols <= 128:
            return first
        return jnp.where(lane < 128 - s, first, pltpu.roll(tiles[t + 1], 128 - s, 1))

    def unpack(ref, source, k):
        lo, size = span(k)
        r, q = source // n_col, lax.rem(source, n_col)
        base = q * (each * all_rows) + r * rows
        tiles = [ref[source, :, lo + at : lo + at + 128].astype(f32) for at in range(0, size, 128)]
        for side, held in ((0, lefts), (1, rights)):
            mine = [t[each * side : each * side + each] for t in tiles]
            for i in range(min(TALL, rows - TALL * k)):
                value = jnp.where(lane < cols, shifted(mine, cols * i), 0.0)
                held[pl.ds(base + TALL * k + i, each, stride=all_rows), :] = value

    def receive(order, send, recv, ssem, rsem):
        for k in order:
            lo, size = span(k)

            def one(s):
                remote(send, recv, ssem, rsem, k, lo, size, s, True).wait_recv()
                unpack(recv, place(s)[1], k)

            peers(one)

    def halved(send, recv, ssem, rsem, k, lo, size, s, arriving, every):
        peer, source, where = place(s)
        slot = source if arriving else me
        return pltpu.make_async_remote_copy(
            src_ref=send.at[lax.rem(peer, h), :, pl.ds(lo, size)],
            dst_ref=recv.at[slot if every else lax.rem(slot, h), :, pl.ds(lo, size)],
            send_sem=ssem.at[k, s], recv_sem=rsem.at[k, s],
            device_id=where, device_id_type=pl.DeviceIdType.MESH,
        )

    lefts_ahead = (send_l, recv_l, ssem_l, rsem_l)
    rights_ahead = (send_r, recv_r, ssem_r, rsem_r)
    sums_back = (send_b, recv_b, ssem_b, rsem_b)

    def unpack_side(ref, slot, source, k, held, span_rows, r):
        lo, size = span(k)
        base = lax.rem(source, n_col) * (wide * span_rows) + r * rows
        tiles = [ref[slot, :, lo + at : lo + at + 128].astype(f32) for at in range(0, size, 128)]
        for part in range(2):
            mine = [t[8 * part : 8 * part + 8] for t in tiles]
            for i in range(min(TALL, rows - TALL * k)):
                value = jnp.where(lane < cols, shifted(mine, cols * i), 0.0)
                held[pl.ds(base + 8 * part * span_rows + TALL * k + i, 8, stride=span_rows), :] = value

    def unpack_left(ref, source, k):
        r = lax.rem(source // n_col, n_row // 2)
        unpack_side(ref, lax.rem(source, h), source, k, lefts, some_rows, r)

    def unpack_right(ref, slot, source, k):
        unpack_side(ref, slot, source, k, rights, all_rows, source // n_col)

    def send_first(k):
        lo, size = span(k)
        peers(lambda s: halved(*rights_ahead, k, lo, size, s, False, True).start())
        near(lambda s: halved(*lefts_ahead, k, lo, size, s, False, False).start())
        unpack_left(send_l, me, k)
        unpack_right(send_r, lax.rem(me, h), me, k)

    def receive_first():
        for k in range(4):
            lo, size = span(k)

            def one_left(s):
                halved(*lefts_ahead, k, lo, size, s, True, False).wait_recv()
                unpack_left(recv_l, place(s)[1], k)

            def one_right(s):
                halved(*rights_ahead, k, lo, size, s, True, True).wait_recv()
                source = place(s)[1]
                unpack_right(recv_r, source, source, k)

            near(one_left)
            peers(one_right)

    def pack_wide(ref, dest, g):
        r, q = lax.rem(dest // n_col, n_row // 2), lax.rem(dest, n_col)
        base = q * (wide * some_rows) + r * rows * wide
        for lo in range(2 * g * step, min(2 * g * step + 2 * step, padded), 128):
            total = jnp.zeros((16, 128), f32)
            for i in range(rows):
                at = i * cols - lo
                if at >= 128 or at + cols <= 0:
                    continue
                value = outs[pl.ds(pl.multiple_of(base + i * wide, 16), wide), :]
                if at % 128:
                    value = pltpu.roll(value, at % 128, 1)
                total = jnp.where((lane_wide >= at) & (lane_wide < at + cols), value, total)
            ref[lax.rem(dest, h), :, lo : lo + 128] = total.astype(bf16)

    def part_of(g):
        return 2 * g * step, min(2 * step, padded - 2 * g * step)

    def give_first():
        for g in range(2):

            def one(s):
                pack_wide(send_b, place(s)[0], g)
                halved(*sums_back, g, *part_of(g), s, False, False).start()

            near(one)
        for g in range(2):
            pack_wide(recv_b, me, g)

    def take_first(g):
        near(lambda s: halved(*sums_back, g, *part_of(g), s, True, False).wait_recv())
        lo, size = part_of(g)
        for at in range(lo, lo + size, 128):
            keep = min(128, cells - at)
            piece = recv_b[:, :, at : at + 128].astype(f32).reshape(h * wide, 128).T
            summed[at : at + keep, :] = piece[:keep]

    def channel(held, q, c, offset, size):
        at = pl.multiple_of(q * (each * all_rows) + c * all_rows + offset, 8)
        return held[pl.ds(at, size), :]

    def outgoing(c, _):
        left = []
        for q in range(n_col):
            at = pl.multiple_of(q * (wide * some_rows) + c * some_rows, 8)
            left.append(lefts[pl.ds(at, some_rows), :].astype(bf16))
        for jq in range(n_col):
            total = None
            for q in range(n_col):
                at = pl.multiple_of(q * (wide * all_rows) + c * all_rows + jq * cols, 8)
                right = rights[pl.ds(at, 128), :].astype(bf16)
                term = lax.dot_general(left[q], right, NT, preferred_element_type=f32)
                total = term if total is None else total + term
            outs[pl.ds(jq * (wide * some_rows) + c, some_rows, stride=wide), :] = total
        return 0

    def incoming(c, _):
        right = [channel(rights, q, c, 0, all_rows).astype(bf16) for q in range(n_col)]
        for iq in range(n_col):
            left = channel(lefts, iq, c, 0, all_rows).T.astype(bf16)
            for jq in range(n_col):
                total = project(left, right[jq])[:cols]
                at = jq * (each * all_rows) + iq * cols * each + c
                outs[pl.ds(at, cols, stride=each), :] = total
        return 0

    def pack(ref, dest, g):
        r, q = dest // n_col, lax.rem(dest, n_col)
        base = q * (each * all_rows) + r * rows * each
        for t in range(step // 128):
            parts = []
            for k in (g, g + 2):
                total = jnp.zeros((8, 128), f32)
                for i in range(min(TALL, rows - TALL * k)):
                    at = i * cols - 128 * t
                    if at >= 128 or at + cols <= 0:
                        continue
                    spot = pl.multiple_of(base + (TALL * k + i) * each, 8)
                    value = outs[pl.ds(spot, each), :]
                    if at % 128:
                        value = pltpu.roll(value, at % 128, 1)
                    total = jnp.where((lane >= at) & (lane < at + cols), value, total)
                parts.append(total)
            lo = g * step + 128 * t
            ref[dest, :, lo : lo + 128] = jnp.concatenate(parts, axis=0).astype(bf16)

    def give_back(send, recv, ssem, rsem):
        for g in range(2):

            def one(s):
                pack(send, place(s)[0], g)
                remote(send, recv, ssem, rsem, g, g * step, step, s, False).start()

            peers(one)
        for g in range(2):
            pack(recv, me, g)

    def take_back(g, send, recv, ssem, rsem):
        peers(lambda s: remote(send, recv, ssem, rsem, g, g * step, step, s, True).wait_recv())
        for t in range(step // 128):
            lo = g * step + 128 * t
            tile = recv[:, :, lo : lo + 128].astype(f32)
            for half in range(2):
                at = (g + 2 * half) * step + 128 * t
                keep = min(128, cells - at)
                if keep > 0:
                    piece = tile[:, each * half : each * half + each, :].reshape(n * each, 128).T
                    summed[at : at + keep, :] = piece[:keep]

    def finish(u, before, lo, size):
        done = normalize(summed[pl.ds(lo, size), :], gains_ref[2 * u + 1 : 2 * u + 2, :]).astype(bf16)
        result = before.astype(f32) + gate[pl.ds(lo, size), :] * project(done, out_w_ref[u])
        return result.astype(bf16)

    def bounds(k):
        return starts[k], min(step, cells - starts[k])

    ahead_b = (send_c, recv_c, ssem_c, rsem_c)
    back_b = (send_d, recv_d, ssem_d, rsem_d)
    for k in range(4):
        lo, size = bounds(k)
        prepare(0, x_ref[lo : lo + size, :].astype(f32), lo, size, (send_l, send_r))
        if k == 0:
            pl.semaphore_wait(barrier, n - 1)
        send_first(k)
    receive_first()
    lax.fori_loop(0, wide, outgoing, 0)
    give_first()
    for g in range(2):
        take_first(g)
        for k in (2 * g, 2 * g + 1):
            lo, size = bounds(k)
            held = finish(0, x_ref[lo : lo + size, :], lo, size)
            mid[lo : lo + size, :] = held
            prepare(1, held.astype(f32), lo, size, send_c)
            send_chunk(k, *ahead_b)
    receive((0, 1, 2, 3), *ahead_b)
    lax.fori_loop(0, each, incoming, 0)
    give_back(*back_b)

    last = step // 2

    def transition(k, _):
        lo = pl.multiple_of(k * last, 16)
        new = finish(1, mid[pl.ds(lo, last), :], lo, last).astype(f32)
        flat = normalize(new, tgain_ref[...]).astype(bf16)
        first = project(flat, up_ref[0])
        inner = (first * jax.nn.sigmoid(first) * project(flat, up_ref[1])).astype(bf16)
        o_ref[pl.ds(lo, last), :] = (new + project(inner, down_ref[...])).astype(bf16)
        return 0

    for g in range(2):
        take_back(g, *back_b)
        for k in (g, g + 2):
            lo, size = bounds(k)
            lax.fori_loop(lo // last, (lo + size) // last, transition, 0)

    def drain(s):
        for k in range(4):
            lo, size = span(k)
            halved(*rights_ahead, k, lo, size, s, True, True).wait_send()
            remote(*ahead_b, k, lo, size, s, True).wait_send()
        for g in range(2):
            remote(*back_b, g, g * step, step, s, True).wait_send()

    def drain_near(s):
        for k in range(4):
            halved(*lefts_ahead, k, *span(k), s, True, False).wait_send()
        for g in range(2):
            halved(*sums_back, g, *part_of(g), s, True, False).wait_send()

    near(drain_near)
    peers(drain)


def fused(n_row, n_col, pair, tri_gains, tri_proj, tri_out, trans_gain, trans_up, trans_down):
    rows, cols, width = pair.shape
    n = n_row * n_col
    cells = rows * cols
    up128 = lambda v: -(-v // 128) * 128
    ahead = pltpu.VMEM((n, 16, up128(cells)), jnp.bfloat16)
    back = pltpu.VMEM((n, 16, 2 * TALL * cols), jnp.bfloat16)
    panel = pltpu.VMEM((n_col * 8 * n_row * rows + 16, 128), jnp.float32)
    panel_big = pltpu.VMEM((n_col * 16 * n_row * rows + 16, 128), jnp.float32)
    ahead_half = pltpu.VMEM((n // 2, 16, up128(cells)), jnp.bfloat16)
    many = pltpu.SemaphoreType.DMA((4, n))
    few = pltpu.SemaphoreType.DMA((2, n))
    whole = pl.BlockSpec(memory_space=pltpu.VMEM)
    out = pl.pallas_call(
        functools.partial(fused_kernel, n_row, n_col, rows, cols),
        out_shape=jax.ShapeDtypeStruct((cells, width), pair.dtype),
        in_specs=[whole] * 7,
        out_specs=whole,
        scratch_shapes=[
            pltpu.VMEM((2, 4 * width, width), jnp.bfloat16),
            pltpu.VMEM((cells, width), jnp.float32),
            pltpu.VMEM((cells, width), jnp.bfloat16),
            pltpu.VMEM((cells, width), jnp.float32),
            panel, panel_big, panel,
            ahead_half, ahead_half, ahead_half, ahead, ahead_half, ahead_half, ahead, ahead, back, back,
            many, many, many, many, few, few, many, many, few, few,
        ],
        compiler_params=pltpu.CompilerParams(
            collective_id=4, has_side_effects=True, vmem_limit_bytes=56 * 1024 * 1024
        ),
        name="fused",
    )(
        pair.reshape(cells, width), tri_gains.reshape(4, width), tri_proj, tri_out,
        trans_gain.reshape(1, width), trans_up, trans_down,
    )
    return out.reshape(rows, cols, width)


def pad_rows(x):
    short = -x.shape[1] % 16
    return jnp.pad(x, ((0, 0), (0, short), (0, 0))) if short else x


def on_device(n_row, n_col, pair, tri_gains, tri_proj, tri_out, trans_gain, trans_up, trans_down):
    rows, cols, width = pair.shape
    n = n_row * n_col
    cells = rows * cols
    each = width // n
    square = n_row * rows == n_col * cols
    if each == 8 and width == 128 and square and n_row % 2 == 0 and cols % 16 == 0 and rows in (28, 32):
        return fused(n_row, n_col, pair, tri_gains, tri_proj, tri_out, trans_gain, trans_up, trans_down)

    def update(pair, gains, weights, out_weight, spec, cid):
        flat = normalize(pair.reshape(-1, width).astype(jnp.float32), gains[0]).astype(jnp.bfloat16)

        def turned(weight):
            return lax.dot_general(weight, flat, (((0,), (1,)), ((), ())), preferred_element_type=jnp.float32)

        left = (jax.nn.sigmoid(turned(weights[1])) * turned(weights[0])).astype(jnp.bfloat16)
        right = (jax.nn.sigmoid(turned(weights[3])) * turned(weights[2])).astype(jnp.bfloat16)
        gate = jax.nn.sigmoid(project(flat, weights[4]))
        both = jnp.concatenate([left.reshape(n, each, cells), right.reshape(n, each, cells)], axis=1)
        both = exchange(pad_rows(both), n_row, n_col, cid)[:, : 2 * each]
        both = both.reshape(n_row, n_col, 2, each, rows, cols)
        both = jnp.transpose(both, (2, 3, 0, 4, 1, 5)).reshape(2, each, n_row * rows, n_col * cols)
        summed = jnp.einsum(spec, both[0], both[1], preferred_element_type=jnp.float32).astype(jnp.bfloat16)
        summed = summed.reshape(each, n_row, rows, n_col, cols)
        summed = jnp.transpose(summed, (1, 3, 0, 2, 4)).reshape(n, 2 * each, cells // 2)
        summed = exchange(pad_rows(summed), n_row, n_col, cid + 1)[:, : 2 * each]
        summed = jnp.transpose(summed.reshape(width, cells), (1, 0)).astype(jnp.float32)
        done = normalize(summed, gains[1]).astype(jnp.bfloat16)
        result = pair.reshape(-1, width).astype(jnp.float32) + gate * project(done, out_weight)
        return result.astype(jnp.bfloat16).reshape(pair.shape)

    pair_mid = update(pair, tri_gains[0], tri_proj[0], tri_out[0], "cik,cjk->cij", 0)
    pair_new = update(pair_mid, tri_gains[1], tri_proj[1], tri_out[1], "cki,ckj->cij", 2)
    flat = normalize(pair_new.reshape(-1, width).astype(jnp.float32), trans_gain).astype(jnp.bfloat16)
    inner = (jax.nn.silu(project(flat, trans_up[0])) * project(flat, trans_up[1])).astype(jnp.bfloat16)
    result = pair_new.reshape(-1, width).astype(jnp.float32) + project(inner, trans_down)
    return result.astype(jnp.bfloat16).reshape(rows, cols, width)


def solution(mesh):
    placed = (P(("rep", "row"), "col", None), P(), P(), P(), P(), P(), P())
    return jax.shard_map(
        functools.partial(on_device, mesh.shape["row"], mesh.shape["col"]),
        mesh=mesh,
        in_specs=placed,
        out_specs=P(("rep", "row"), "col", None),
        check_vma=False,
    )
```

```python
import functools

import jax
import jax.numpy as jnp
from jax import lax
from jax.experimental import pallas as pl
from jax.experimental.pallas import tpu as pltpu
from jax.sharding import PartitionSpec as P

GROUP = ("row", "col")


def normalize(values, gain):
    mean = jnp.mean(values, axis=-1, keepdims=True)
    centered = values - mean
    variance = jnp.mean(centered * centered, axis=-1, keepdims=True)
    return centered * lax.rsqrt(variance + 1e-05) * gain


def project(flat, weight):
    return jnp.dot(flat, weight, preferred_element_type=jnp.float32)


def exchange_kernel(n_row, n_col, x_ref, o_ref, send_sem, recv_sem, local_sem):
    n = n_row * n_col
    me = lax.axis_index("row") * n_col + lax.axis_index("col")

    def place(d):
        peer = lax.rem(me + d, n)
        return peer, {"row": peer // n_col, "col": lax.rem(peer, n_col)}

    barrier = pltpu.get_barrier_semaphore()

    def greet(d, _):
        pl.semaphore_signal(barrier, inc=1, device_id=place(d)[1], device_id_type=pl.DeviceIdType.MESH)
        return 0

    lax.fori_loop(1, n, greet, 0)
    own = pltpu.make_async_copy(x_ref.at[me], o_ref.at[me], local_sem)
    own.start()
    pl.semaphore_wait(barrier, n - 1)

    def send(d, _):
        peer, where = place(d)
        pltpu.make_async_remote_copy(
            src_ref=x_ref.at[peer], dst_ref=o_ref.at[me],
            send_sem=send_sem.at[d], recv_sem=recv_sem.at[d],
            device_id=where, device_id_type=pl.DeviceIdType.MESH,
        ).start()
        return 0

    lax.fori_loop(1, n, send, 0)

    def finish(d, _):
        peer, where = place(d)
        source = lax.rem(me - d + n, n)
        copy = pltpu.make_async_remote_copy(
            src_ref=x_ref.at[peer], dst_ref=o_ref.at[source],
            send_sem=send_sem.at[d], recv_sem=recv_sem.at[d],
            device_id=where, device_id_type=pl.DeviceIdType.MESH,
        )
        copy.wait_send()
        copy.wait_recv()
        return 0

    lax.fori_loop(1, n, finish, 0)
    own.wait()


def exchange(x, n_row, n_col, cid):
    n = n_row * n_col
    return pl.pallas_call(
        functools.partial(exchange_kernel, n_row, n_col),
        out_shape=jax.ShapeDtypeStruct(x.shape, x.dtype),
        in_specs=[pl.BlockSpec(memory_space=pltpu.VMEM)],
        out_specs=pl.BlockSpec(memory_space=pltpu.VMEM),
        scratch_shapes=[
            pltpu.SemaphoreType.DMA((n,)),
            pltpu.SemaphoreType.DMA((n,)),
            pltpu.SemaphoreType.DMA,
        ],
        compiler_params=pltpu.CompilerParams(
            collective_id=cid, has_side_effects=True, vmem_limit_bytes=40 * 1024 * 1024
        ),
        name=f"exchange_{cid}",
    )(x)


NT = (((1,), (1,)), ((), ()))
TALL = 8


def fused_kernel(
    n_row, n_col, rows, cols,
    x_ref, gains_ref, proj_ref, out_w_ref, tgain_ref, up_ref, down_ref, o_ref,
    turned, gate, mid, summed, lefts, rights, outs,
    send_l, recv_l, send_r, recv_r, send_b, recv_b, send_c, recv_c, send_d, recv_d,
    ssem_l, rsem_l, ssem_r, rsem_r, ssem_b, rsem_b, ssem_c, rsem_c, ssem_d, rsem_d,
):
    n = n_row * n_col
    cells = rows * cols
    each = 8
    all_rows = n_row * rows
    step = TALL * cols
    h = n // 2
    row = lax.axis_index("row")
    col = lax.axis_index("col")
    me = row * n_col + col
    f32, bf16 = jnp.float32, jnp.bfloat16
    starts = list(range(0, cells, step))
    padded = send_c.shape[2]
    wide = 2 * each
    some_rows = all_rows // 2
    lane_wide = lax.broadcasted_iota(jnp.int32, (16, 128), 1)
    lane = lax.broadcasted_iota(jnp.int32, (8, 128), 1)

    def place(s):
        side = lax.rem(me // h + 1 + s // h, 2)
        peer = side * h + lax.rem(lax.rem(me, h) + s, h)
        source = side * h + lax.rem(lax.rem(me, h) + n - s, h)
        return peer, source, {"row": peer // n_col, "col": lax.rem(peer, n_col)}

    def peers(body):
        def one(s, _):
            body(s)
            return 0

        lax.fori_loop(0, h, one, 0)
        lax.fori_loop(h + 1, n, one, 0)

    def near(body):
        def one(s, _):
            body(s)
            return 0

        lax.fori_loop(h + 1, n, one, 0)

    barrier = pltpu.get_barrier_semaphore()

    def greet(s):
        pl.semaphore_signal(barrier, inc=1, device_id=place(s)[2], device_id_type=pl.DeviceIdType.MESH)

    peers(greet)

    for u in range(2):
        for m in range(4):
            turned[u, m * 128 : (m + 1) * 128, :] = proj_ref[u, m].astype(f32).T.astype(bf16)
    tail = cells - cells // 128 * 128
    if tail:
        zero = jnp.zeros((n, 16, 128), bf16)
        send_l[:, :, padded - 128 :] = zero[:h]
        send_r[:, :, padded - 128 :] = zero[:h]
        send_c[:, :, padded - 128 :] = zero

    def remote(send, recv, ssem, rsem, k, lo, size, s, arriving):
        peer, source, where = place(s)
        return pltpu.make_async_remote_copy(
            src_ref=send.at[peer, :, pl.ds(lo, size)],
            dst_ref=recv.at[source if arriving else me, :, pl.ds(lo, size)],
            send_sem=ssem.at[k, s], recv_sem=rsem.at[k, s],
            device_id=where, device_id_type=pl.DeviceIdType.MESH,
        )

    def span(k):
        lo = starts[k]
        return lo, (padded if k == len(starts) - 1 else lo + step) - lo

    def prepare(u, values, lo, size, send):
        flat = normalize(values, gains_ref[2 * u : 2 * u + 1, :]).astype(bf16)
        gate[lo : lo + size, :] = jax.nn.sigmoid(project(flat, proj_ref[u, 4]))
        for side in range(2):
            value = lax.dot_general(
                turned[u, 256 * side : 256 * side + 128, :], flat, NT, preferred_element_type=f32
            )
            scale = lax.dot_general(
                turned[u, 256 * side + 128 : 256 * side + 256, :], flat, NT, preferred_element_type=f32
            )
            held = (jax.nn.sigmoid(scale) * value).astype(bf16)
            if u == 0:
                send[side][:, :, lo : lo + size] = held.reshape(h, wide, size)
            else:
                send[:, each * side : each * side + each, lo : lo + size] = held.reshape(n, each, size)

    def send_chunk(k, send, recv, ssem, rsem):
        lo, size = span(k)
        peers(lambda s: remote(send, recv, ssem, rsem, k, lo, size, s, False).start())
        unpack(send, me, k)

    def shifted(tiles, start):
        t, s = start // 128, start % 128
        if s == 0:
            return tiles[t]
        first = pltpu.roll(tiles[t], 128 - s, 1)
        if s + cols <= 128:
            return first
        return jnp.where(lane < 128 - s, first, pltpu.roll(tiles[t + 1], 128 - s, 1))

    def unpack(ref, source, k):
        lo, size = span(k)
        r, q = source // n_col, lax.rem(source, n_col)
        base = q * (each * all_rows) + r * rows
        tiles = [ref[source, :, lo + at : lo + at + 128].astype(f32) for at in range(0, size, 128)]
        for side, held in ((0, lefts), (1, rights)):
            mine = [t[each * side : each * side + each] for t in tiles]
            for i in range(min(TALL, rows - TALL * k)):
                value = jnp.where(lane < cols, shifted(mine, cols * i), 0.0)
                held[pl.ds(base + TALL * k + i, each, stride=all_rows), :] = value

    def receive(order, send, recv, ssem, rsem):
        for k in order:
            lo, size = span(k)

            def one(s):
                remote(send, recv, ssem, rsem, k, lo, size, s, True).wait_recv()
                unpack(recv, place(s)[1], k)

            peers(one)

    def halved(send, recv, ssem, rsem, k, lo, size, s, arriving, every):
        peer, source, where = place(s)
        slot = source if arriving else me
        return pltpu.make_async_remote_copy(
            src_ref=send.at[lax.rem(peer, h), :, pl.ds(lo, size)],
            dst_ref=recv.at[slot if every else lax.rem(slot, h), :, pl.ds(lo, size)],
            send_sem=ssem.at[k, s], recv_sem=rsem.at[k, s],
            device_id=where, device_id_type=pl.DeviceIdType.MESH,
        )

    lefts_ahead = (send_l, recv_l, ssem_l, rsem_l)
    rights_ahead = (send_r, recv_r, ssem_r, rsem_r)
    sums_back = (send_b, recv_b, ssem_b, rsem_b)

    def unpack_side(ref, slot, source, k, held, span_rows, r):
        lo, size = span(k)
        base = lax.rem(source, n_col) * (wide * span_rows) + r * rows
        tiles = [ref[slot, :, lo + at : lo + at + 128].astype(f32) for at in range(0, size, 128)]
        for part in range(2):
            mine = [t[8 * part : 8 * part + 8] for t in tiles]
            for i in range(min(TALL, rows - TALL * k)):
                value = jnp.where(lane < cols, shifted(mine, cols * i), 0.0)
                held[pl.ds(base + 8 * part * span_rows + TALL * k + i, 8, stride=span_rows), :] = value

    def unpack_left(ref, source, k):
        r = lax.rem(source // n_col, n_row // 2)
        unpack_side(ref, lax.rem(source, h), source, k, lefts, some_rows, r)

    def unpack_right(ref, slot, source, k):
        unpack_side(ref, slot, source, k, rights, all_rows, source // n_col)

    def send_first(k):
        lo, size = span(k)
        peers(lambda s: halved(*rights_ahead, k, lo, size, s, False, True).start())
        near(lambda s: halved(*lefts_ahead, k, lo, size, s, False, False).start())
        unpack_left(send_l, me, k)
        unpack_right(send_r, lax.rem(me, h), me, k)

    def receive_first():
        for k in range(4):
            lo, size = span(k)

            def one_left(s):
                halved(*lefts_ahead, k, lo, size, s, True, False).wait_recv()
                unpack_left(recv_l, place(s)[1], k)

            def one_right(s):
                halved(*rights_ahead, k, lo, size, s, True, True).wait_recv()
                source = place(s)[1]
                unpack_right(recv_r, source, source, k)

            near(one_left)
            peers(one_right)

    def pack_wide(ref, dest, g):
        r, q = lax.rem(dest // n_col, n_row // 2), lax.rem(dest, n_col)
        base = q * (wide * some_rows) + r * rows * wide
        for lo in range(2 * g * step, min(2 * g * step + 2 * step, padded), 128):
            total = jnp.zeros((16, 128), f32)
            for i in range(rows):
                at = i * cols - lo
                if at >= 128 or at + cols <= 0:
                    continue
                value = outs[pl.ds(pl.multiple_of(base + i * wide, 16), wide), :]
                if at % 128:
                    value = pltpu.roll(value, at % 128, 1)
                total = jnp.where((lane_wide >= at) & (lane_wide < at + cols), value, total)
            ref[lax.rem(dest, h), :, lo : lo + 128] = total.astype(bf16)

    def part_of(g):
        return 2 * g * step, min(2 * step, padded - 2 * g * step)

    def give_first():
        for g in range(2):

            def one(s):
                pack_wide(send_b, place(s)[0], g)
                halved(*sums_back, g, *part_of(g), s, False, False).start()

            near(one)
        for g in range(2):
            pack_wide(recv_b, me, g)

    def take_first(g):
        near(lambda s: halved(*sums_back, g, *part_of(g), s, True, False).wait_recv())
        lo, size = part_of(g)
        for at in range(lo, lo + size, 128):
            keep = min(128, cells - at)
            piece = recv_b[:, :, at : at + 128].astype(f32).reshape(h * wide, 128).T
            summed[at : at + keep, :] = piece[:keep]

    def channel(held, q, c, offset, size):
        at = pl.multiple_of(q * (each * all_rows) + c * all_rows + offset, 8)
        return held[pl.ds(at, size), :]

    def outgoing(c, _):
        left = []
        for q in range(n_col):
            at = pl.multiple_of(q * (wide * some_rows) + c * some_rows, 8)
            left.append(lefts[pl.ds(at, some_rows), :].astype(bf16))
        for jq in range(n_col):
            total = None
            for q in range(n_col):
                at = pl.multiple_of(q * (wide * all_rows) + c * all_rows + jq * cols, 8)
                right = rights[pl.ds(at, 128), :].astype(bf16)
                term = lax.dot_general(left[q], right, NT, preferred_element_type=f32)
                total = term if total is None else total + term
            outs[pl.ds(jq * (wide * some_rows) + c, some_rows, stride=wide), :] = total
        return 0

    def incoming(c, _):
        right = [channel(rights, q, c, 0, all_rows).astype(bf16) for q in range(n_col)]
        for iq in range(n_col):
            left = channel(lefts, iq, c, 0, all_rows).T.astype(bf16)
            for jq in range(n_col):
                total = project(left, right[jq])[:cols]
                at = jq * (each * all_rows) + iq * cols * each + c
                outs[pl.ds(at, cols, stride=each), :] = total
        return 0

    def fold(g):
        tall = (rows - 2 * TALL) // 2 if g else TALL
        return tall, -(-tall * cols // 128) * 128

    def pack(ref, dest, g):
        r, q = dest // n_col, lax.rem(dest, n_col)
        base = q * (each * all_rows) + r * rows * each
        tall, width = fold(g)
        for t in range(width // 128):
            parts = []
            for half in range(2):
                total = jnp.zeros((8, 128), f32)
                for i in range(tall):
                    at = i * cols - 128 * t
                    if at >= 128 or at + cols <= 0:
                        continue
                    spot = pl.multiple_of(base + (2 * TALL * g + half * tall + i) * each, 8)
                    value = outs[pl.ds(spot, each), :]
                    if at % 128:
                        value = pltpu.roll(value, at % 128, 1)
                    total = jnp.where((lane >= at) & (lane < at + cols), value, total)
                parts.append(total)
            lo = g * step + 128 * t
            ref[dest, :, lo : lo + 128] = jnp.concatenate(parts, axis=0).astype(bf16)

    def give_back(send, recv, ssem, rsem):
        for g in range(2):

            def one(s):
                pack(send, place(s)[0], g)
                remote(send, recv, ssem, rsem, g, g * step, fold(g)[1], s, False).start()

            peers(one)
        for g in range(2):
            pack(recv, me, g)

    def take_back(g, send, recv, ssem, rsem):
        peers(lambda s: remote(send, recv, ssem, rsem, g, g * step, fold(g)[1], s, True).wait_recv())
        tall, width = fold(g)
        for t in range(width // 128):
            lo = g * step + 128 * t
            tile = recv[:, :, lo : lo + 128].astype(f32)
            for half in range(2):
                at = (2 * TALL * g + half * tall) * cols + 128 * t
                keep = min(128, tall * cols - 128 * t)
                if keep > 0:
                    piece = tile[:, each * half : each * half + each, :].reshape(n * each, 128).T
                    summed[at : at + keep, :] = piece[:keep]

    def finish(u, before, lo, size):
        done = normalize(summed[pl.ds(lo, size), :], gains_ref[2 * u + 1 : 2 * u + 2, :]).astype(bf16)
        result = before.astype(f32) + gate[pl.ds(lo, size), :] * project(done, out_w_ref[u])
        return result.astype(bf16)

    def bounds(k):
        return starts[k], min(step, cells - starts[k])

    ahead_b = (send_c, recv_c, ssem_c, rsem_c)
    back_b = (send_d, recv_d, ssem_d, rsem_d)
    for k in range(4):
        lo, size = bounds(k)
        prepare(0, x_ref[lo : lo + size, :].astype(f32), lo, size, (send_l, send_r))
        if k == 0:
            pl.semaphore_wait(barrier, n - 1)
        send_first(k)
    receive_first()
    lax.fori_loop(0, wide, outgoing, 0)
    give_first()
    for g in range(2):
        take_first(g)
        for k in (2 * g, 2 * g + 1):
            lo, size = bounds(k)
            held = finish(0, x_ref[lo : lo + size, :], lo, size)
            mid[lo : lo + size, :] = held
            prepare(1, held.astype(f32), lo, size, send_c)
            send_chunk(k, *ahead_b)
    receive((0, 1, 2, 3), *ahead_b)
    lax.fori_loop(0, each, incoming, 0)
    give_back(*back_b)

    last = step // 2

    def transition(k, _):
        lo = pl.multiple_of(k * last, 16)
        new = finish(1, mid[pl.ds(lo, last), :], lo, last).astype(f32)
        flat = normalize(new, tgain_ref[...]).astype(bf16)
        first = project(flat, up_ref[0])
        inner = (first * jax.nn.sigmoid(first) * project(flat, up_ref[1])).astype(bf16)
        o_ref[pl.ds(lo, last), :] = (new + project(inner, down_ref[...])).astype(bf16)
        return 0

    for g in range(2):
        take_back(g, *back_b)
        for k in (2 * g, 2 * g + 1):
            lo, size = bounds(k)
            lax.fori_loop(lo // last, (lo + size) // last, transition, 0)

    def drain(s):
        for k in range(4):
            lo, size = span(k)
            halved(*rights_ahead, k, lo, size, s, True, True).wait_send()
            remote(*ahead_b, k, lo, size, s, True).wait_send()
        for g in range(2):
            remote(*back_b, g, g * step, fold(g)[1], s, True).wait_send()

    def drain_near(s):
        for k in range(4):
            halved(*lefts_ahead, k, *span(k), s, True, False).wait_send()
        for g in range(2):
            halved(*sums_back, g, *part_of(g), s, True, False).wait_send()

    near(drain_near)
    peers(drain)


def fused(n_row, n_col, pair, tri_gains, tri_proj, tri_out, trans_gain, trans_up, trans_down):
    rows, cols, width = pair.shape
    n = n_row * n_col
    cells = rows * cols
    up128 = lambda v: -(-v // 128) * 128
    ahead = pltpu.VMEM((n, 16, up128(cells)), jnp.bfloat16)
    back = pltpu.VMEM((n, 16, 2 * TALL * cols), jnp.bfloat16)
    panel = pltpu.VMEM((n_col * 8 * n_row * rows + 16, 128), jnp.float32)
    panel_big = pltpu.VMEM((n_col * 16 * n_row * rows + 16, 128), jnp.float32)
    ahead_half = pltpu.VMEM((n // 2, 16, up128(cells)), jnp.bfloat16)
    many = pltpu.SemaphoreType.DMA((4, n))
    few = pltpu.SemaphoreType.DMA((2, n))
    whole = pl.BlockSpec(memory_space=pltpu.VMEM)
    out = pl.pallas_call(
        functools.partial(fused_kernel, n_row, n_col, rows, cols),
        out_shape=jax.ShapeDtypeStruct((cells, width), pair.dtype),
        in_specs=[whole] * 7,
        out_specs=whole,
        scratch_shapes=[
            pltpu.VMEM((2, 4 * width, width), jnp.bfloat16),
            pltpu.VMEM((cells, width), jnp.float32),
            pltpu.VMEM((cells, width), jnp.bfloat16),
            pltpu.VMEM((cells, width), jnp.float32),
            panel, panel_big, panel,
            ahead_half, ahead_half, ahead_half, ahead, ahead_half, ahead_half, ahead, ahead, back, back,
            many, many, many, many, few, few, many, many, few, few,
        ],
        compiler_params=pltpu.CompilerParams(
            collective_id=4, has_side_effects=True, vmem_limit_bytes=56 * 1024 * 1024
        ),
        name="fused",
    )(
        pair.reshape(cells, width), tri_gains.reshape(4, width), tri_proj, tri_out,
        trans_gain.reshape(1, width), trans_up, trans_down,
    )
    return out.reshape(rows, cols, width)


def pad_rows(x):
    short = -x.shape[1] % 16
    return jnp.pad(x, ((0, 0), (0, short), (0, 0))) if short else x


def on_device(n_row, n_col, pair, tri_gains, tri_proj, tri_out, trans_gain, trans_up, trans_down):
    rows, cols, width = pair.shape
    n = n_row * n_col
    cells = rows * cols
    each = width // n
    square = n_row * rows == n_col * cols
    if each == 8 and width == 128 and square and n_row % 2 == 0 and cols % 16 == 0 and rows in (28, 32):
        return fused(n_row, n_col, pair, tri_gains, tri_proj, tri_out, trans_gain, trans_up, trans_down)

    def update(pair, gains, weights, out_weight, spec, cid):
        flat = normalize(pair.reshape(-1, width).astype(jnp.float32), gains[0]).astype(jnp.bfloat16)

        def turned(weight):
            return lax.dot_general(weight, flat, (((0,), (1,)), ((), ())), preferred_element_type=jnp.float32)

        left = (jax.nn.sigmoid(turned(weights[1])) * turned(weights[0])).astype(jnp.bfloat16)
        right = (jax.nn.sigmoid(turned(weights[3])) * turned(weights[2])).astype(jnp.bfloat16)
        gate = jax.nn.sigmoid(project(flat, weights[4]))
        both = jnp.concatenate([left.reshape(n, each, cells), right.reshape(n, each, cells)], axis=1)
        both = exchange(pad_rows(both), n_row, n_col, cid)[:, : 2 * each]
        both = both.reshape(n_row, n_col, 2, each, rows, cols)
        both = jnp.transpose(both, (2, 3, 0, 4, 1, 5)).reshape(2, each, n_row * rows, n_col * cols)
        summed = jnp.einsum(spec, both[0], both[1], preferred_element_type=jnp.float32).astype(jnp.bfloat16)
        summed = summed.reshape(each, n_row, rows, n_col, cols)
        summed = jnp.transpose(summed, (1, 3, 0, 2, 4)).reshape(n, 2 * each, cells // 2)
        summed = exchange(pad_rows(summed), n_row, n_col, cid + 1)[:, : 2 * each]
        summed = jnp.transpose(summed.reshape(width, cells), (1, 0)).astype(jnp.float32)
        done = normalize(summed, gains[1]).astype(jnp.bfloat16)
        result = pair.reshape(-1, width).astype(jnp.float32) + gate * project(done, out_weight)
        return result.astype(jnp.bfloat16).reshape(pair.shape)

    pair_mid = update(pair, tri_gains[0], tri_proj[0], tri_out[0], "cik,cjk->cij", 0)
    pair_new = update(pair_mid, tri_gains[1], tri_proj[1], tri_out[1], "cki,ckj->cij", 2)
    flat = normalize(pair_new.reshape(-1, width).astype(jnp.float32), trans_gain).astype(jnp.bfloat16)
    inner = (jax.nn.silu(project(flat, trans_up[0])) * project(flat, trans_up[1])).astype(jnp.bfloat16)
    result = pair_new.reshape(-1, width).astype(jnp.float32) + project(inner, trans_down)
    return result.astype(jnp.bfloat16).reshape(rows, cols, width)


def solution(mesh):
    placed = (P(("rep", "row"), "col", None), P(), P(), P(), P(), P(), P())
    return jax.shard_map(
        functools.partial(on_device, mesh.shape["row"], mesh.shape["col"]),
        mesh=mesh,
        in_specs=placed,
        out_specs=P(("rep", "row"), "col", None),
        check_vma=False,
    )
```
